32 devices in a mesh: groups: 2 (over y), bond: 4 (over z), mpo: 2 (over x), phys: 2 (over core).
Axes of the slice: x: 2, y: 2, z: 4, core: 2. Of those that a mesh axis runs over, the one named last changes fastest.
Arguments:
- psi: bfloat16 [256, 4, 128, 128], P(('groups', 'bond', 'phys')), parts along dimension 0, may hold values from -6 to 6
- left_env: bfloat16 [4, 16, 128, 128], P('mpo', ('groups', 'bond')), parts along dimension 1, may hold values from -0.5 to 0.5
- right_env: bfloat16 [4, 32, 128, 128], P('mpo', ('groups', 'bond')), parts along dimension 1, may hold values from -0.5 to 0.5
- mpo_ops: float32 [4, 4, 4], P('mpo'), may hold values from -3 to 3
- mpo_pattern: int32 [4, 4, 4], P('mpo'), may hold values 0 or 1
- left_mask: int32 [4, 16], P('mpo', 'groups'), parts along dimension 1, may hold values 0 or 1
- right_mask: int32 [4, 32], P('mpo', 'groups'), parts along dimension 1, may hold values 0 or 1
- left_sector: int32 [256], P('groups'), parts along dimension 0, may hold values from 0 to 7, as said below
- right_sector: int32 [256], P('groups'), parts along dimension 0, may hold values from 0 to 15, as said below
- left_size: int32 [16], P('groups'), parts along dimension 0, may hold values from 64 to 128
- right_size: int32 [32], P('groups'), parts along dimension 0, may hold values from 64 to 128
Outputs:
- h_psi: bfloat16 [256, 4, 128, 128], P(('groups', 'bond', 'phys'), None, 'mpo'), parts along dimension 0
The draws below stay inside these ranges and needn't reach their ends.
There are 2 independent parts, one for each index of `groups`. The reference program is written for one: setup_inputs(seed, part) draws one part's arguments, and reference() takes and returns one part's arrays. A program takes and returns all parts, laid end to end along the dimension named above; an argument that names none is the same for every part. Nothing has to cross between parts.
Inputs may be any that keep to these rules, and one draw needn't show every extreme that they name: `left_sector`: blocks are ordered by device: index i of bond holds one aligned run of blocks, 16 on each index of phys in turn, and every block of that run has a left sector from i * 2 to i * 2 + 1. `right_sector`: the owner of right sector r is index r // 4 of bond. Within each aligned run of 16 blocks no owner is named by more than 4 blocks, and one owner is named exactly 4 times in every run.
All inputs are finite; a program needn't handle non-finite values. No bound on the sum of `mpo_pattern` or of `left_mask` or of `right_mask` on one device may be relied on, other than what follows from the above.
Results may differ from the reference program's by a relative error of at most 0.0095.
Values may be sent and summed in bfloat16 or wider, within the bound.
A program may use at most 64 MiB of HBM per device.

```python
import jax
import jax.numpy as jnp
from jax import lax

SEC = 128
PH = 4
KD = 2
LEFT_BOND_SECTORS = 2
SRD = 4
DEVICE_BLOCKS = 16
TOTAL_BLOCKS = 128
K = 4
LEFT_SECTORS = 8
NSEC_R = 16
N_MPO = 2


def draw_left_sector(key, part):
    key = jax.random.fold_in(key, 23)
    lane_slots = TOTAL_BLOCKS // DEVICE_BLOCKS
    blocks_per_owner = lane_slots // (LEFT_SECTORS // LEFT_BOND_SECTORS)
    block_owner = jnp.arange(lane_slots, dtype=jnp.int32) // blocks_per_owner
    inner_part = jax.random.randint(key, (lane_slots, DEVICE_BLOCKS), 0, LEFT_BOND_SECTORS)
    return (block_owner[:, None] * LEFT_BOND_SECTORS + inner_part).reshape(TOTAL_BLOCKS).astype(jnp.int32)


def draw_right_sector(key, part):
    key = jax.random.fold_in(key, 17)
    first, second, third, fourth = jax.random.split(key, 4)
    owners = NSEC_R // SRD
    lane_slots = TOTAL_BLOCKS // DEVICE_BLOCKS
    copies = (DEVICE_BLOCKS + owners - 1) // owners
    preferred_owner = jax.random.randint(first, (), 0, owners)
    owner_ranking = jax.random.permutation(second, owners).astype(jnp.int32)
    random_jitter = jax.random.randint(third, (lane_slots, owners, copies), 0, 4096)
    owner_indices = jnp.arange(owners, dtype=jnp.int32)
    extra_reward = owner_ranking * 256 + jnp.where(owner_indices == preferred_owner, 4194304, 0)
    owner_score = random_jitter + extra_reward[None, :, None]
    flat = owner_score.reshape(lane_slots, owners * copies) * (owners * copies) + jnp.arange(owners * copies, dtype=jnp.int32)[None, :]
    _, picked = lax.top_k(flat, DEVICE_BLOCKS)
    block_owner = picked.astype(jnp.int32) // copies
    inner_part = jax.random.randint(fourth, (lane_slots, DEVICE_BLOCKS), 0, SRD)
    return (block_owner * SRD + inner_part).reshape(TOTAL_BLOCKS).astype(jnp.int32)


def draw_left_size(key, part):
    key = jax.random.fold_in(key, 29)
    sizes = jax.random.randint(key, (LEFT_SECTORS,), SEC // 2, SEC + 1)
    return sizes.at[0].set(SEC).at[1].set(SEC // 2).astype(jnp.int32)


def draw_right_size(key, part):
    key = jax.random.fold_in(key, 31)
    sizes = jax.random.randint(key, (NSEC_R,), SEC // 2, SEC + 1)
    return sizes.at[0].set(SEC).at[1].set(SEC // 2).astype(jnp.int32)


def touch_ends(result, stream_key, least, largest):
    longest = result.shape.index(max(result.shape))
    spots = []
    for shift in (0, 1):
        where = [jax.random.randint(jax.random.fold_in(stream_key, axis), (), 0, length) for axis, length in enumerate(result.shape)]
        where[longest] = (where[longest] + shift) % result.shape[longest]
        spots.append(tuple(where))
    return result.at[spots[0]].set(least).at[spots[1]].set(largest)


def block_levels(stream_key, dims, pieces, low, top_value):
    def one(axis_at, parts):
        draws = jax.random.uniform(jax.random.fold_in(jax.random.fold_in(stream_key, 6), axis_at), (parts,), jnp.float32, low / len(pieces), top_value / len(pieces))
        return jnp.repeat(jnp.exp(draws), dims[axis_at] // parts).reshape((-1,) + (1,) * (len(dims) - axis_at - 1))

    gain = one(*pieces[0])
    for cut in pieces[1:]:
        gain = gain * one(*cut)
    return gain


def centred(key, dims, scale, reach, cuts=(), held_as=jnp.bfloat16):
    entries = scale * jax.random.normal(key, dims, jnp.float32)
    if cuts:
        entries = entries * block_levels(key, dims, cuts, -0.22, 0.18)
    return jnp.clip(entries, -reach, reach).astype(held_as)


def setup_inputs(seed: int = 0, part: int = 0) -> dict:
    seeds = jax.random.split(jax.random.key(seed), 12)
    own_keys = jax.random.split(jax.random.fold_in(seeds[11], part), 12)
    return {
        "psi": centred(own_keys[0], (TOTAL_BLOCKS, PH, SEC, SEC), 1.0, 6.0, ((0, 8),)),
        "left_env": centred(own_keys[1], (K, LEFT_SECTORS, SEC, SEC), SEC ** -0.5, 0.5, ((0, 2), (1, 4))),
        "right_env": centred(own_keys[2], (K, NSEC_R, SEC, SEC), SEC ** -0.5, 0.5, ((0, 2), (1, 4))),
        "mpo_ops": centred(seeds[3], (K, PH, PH), 0.5, 3.0, ((0, 2),), jnp.float32),
        "mpo_pattern": touch_ends((jax.random.randint(seeds[4], (K, PH, PH), 0, 4) < 3).astype(jnp.int32), jax.random.fold_in(seeds[4], 1), 0, 1),
        "left_mask": touch_ends((jax.random.randint(own_keys[5], (K, LEFT_SECTORS), 0, 4) < 3).astype(jnp.int32), jax.random.fold_in(own_keys[5], 1), 0, 1),
        "right_mask": touch_ends((jax.random.randint(own_keys[6], (K, NSEC_R), 0, 4) < 3).astype(jnp.int32), jax.random.fold_in(own_keys[6], 1), 0, 1),
        "left_sector": draw_left_sector(jax.random.fold_in(jax.random.fold_in(seeds[11], part), 71), part),
        "right_sector": draw_right_sector(jax.random.fold_in(jax.random.fold_in(seeds[11], part), 71), part),
        "left_size": draw_left_size(jax.random.fold_in(jax.random.fold_in(seeds[11], part), 71), part),
        "right_size": draw_right_size(jax.random.fold_in(jax.random.fold_in(seeds[11], part), 71), part),
    }


def reference(psi, left_env, right_env, mpo_ops, mpo_pattern, left_mask, right_mask, left_sector, right_sector, left_size, right_size):
    operators = mpo_ops * mpo_pattern.astype(jnp.float32)
    left_keep = left_mask.astype(jnp.float32)
    right_keep = right_mask.astype(jnp.float32)
    positions = jnp.arange(SEC)

    def one_block(inputs):
        block, left_id, right_id = inputs
        row_keep = (positions < left_size[left_id]).astype(jnp.float32)
        col_keep = (positions < right_size[right_id]).astype(jnp.float32)
        keep = row_keep[None, :, None] * col_keep[None, None, :]
        masked = (block.astype(jnp.float32) * keep).astype(jnp.bfloat16)
        left_blocks = jnp.take(left_env, left_id, axis=1).astype(jnp.float32)
        right_blocks = jnp.take(right_env, right_id, axis=1).astype(jnp.float32)
        product = jnp.einsum("kab,sbc->ksac", left_blocks, masked.astype(jnp.float32))
        combined = jnp.einsum("kst,ktac->ksac", operators, product, precision=lax.Precision.HIGHEST)
        weights = left_keep[:, left_id] * right_keep[:, right_id]
        mixed = (combined * weights[:, None, None, None]).astype(jnp.bfloat16)
        terms = jnp.einsum("ksab,kbc->ksac", mixed.astype(jnp.float32), right_blocks)
        grouped = jnp.sum(terms.reshape(N_MPO, KD, PH, SEC, SEC), axis=1)
        rounded = lax.optimization_barrier(grouped.astype(jnp.bfloat16)).astype(jnp.float32)
        total = jnp.sum(rounded, axis=0)
        return (total * keep).astype(jnp.bfloat16)

    return lax.map(one_block, (psi, left_sector, right_sector))
```

```python
import functools

import jax
import jax.numpy as jnp
from jax import lax
from jax.experimental import pallas as pl
from jax.experimental.pallas import tpu as pltpu
from jax.sharding import PartitionSpec as P

MESH = pl.DeviceIdType.MESH


def loop(count, body):
    if count <= 8:
        for index in range(count):
            body(index)
    else:
        lax.fori_loop(0, count, lambda i, c: (body(i), c)[1], 0)


def kernel(
    sizes,
    psi_ref,
    left_ref,
    right_ref,
    ops_ref,
    pat_ref,
    lmask_ref,
    rmask_ref,
    lsec,
    rsec,
    lsize,
    rsize,
    out_ref,
    psi_v,
    left_v,
    left_all,
    right_own,
    right_oth,
    mix,
    acc,
    out_v,
    ops_all,
    pat_all,
    lmask_all,
    rmask_all,
    coef,
    psi_sem,
    out_sem,
    own_sem,
    small_send,
    small_recv,
    z_send,
    z_recv,
    x_send,
    x_recv,
    cz_send,
    cz_recv,
    cx_send,
    cx_recv,
):
    n_b, n_m, n_p = sizes
    blocks, states, width, _ = psi_ref.shape
    terms = left_ref.shape[0]
    lcount = left_ref.shape[1]
    rcount = right_ref.shape[1]
    rows = width // n_m
    piece = rcount // n_p
    here = lax.axis_index("bond")
    mine = lax.axis_index("mpo")
    lane = lax.axis_index("phys")
    chunks = psi_sem.shape[0]
    per = blocks // chunks

    psi_copies = [
        pltpu.make_async_copy(
            psi_ref.at[pl.ds(c * per, per)], psi_v.at[pl.ds(c * per, per)], psi_sem.at[c]
        )
        for c in range(chunks)
    ]
    own_copies = [
        pltpu.make_async_copy(
            left_ref.at[:, :, pl.ds(mine * rows, rows)], left_v.at[0], own_sem.at[0]
        ),
        pltpu.make_async_copy(
            right_ref, right_own.at[:, pl.ds(here * rcount, rcount)], own_sem.at[1]
        ),
        pltpu.make_async_copy(ops_ref, ops_all.at[0], own_sem.at[2]),
        pltpu.make_async_copy(pat_ref, pat_all.at[0], own_sem.at[3]),
        pltpu.make_async_copy(lmask_ref, lmask_all.at[0], own_sem.at[4]),
        pltpu.make_async_copy(rmask_ref, rmask_all.at[0], own_sem.at[5]),
    ]
    for copy in own_copies + psi_copies:
        copy.start()

    def b_peer(d):
        return lax.rem(here + d, n_b)

    def b_from(d):
        return lax.rem(here + n_b - d, n_b)

    def m_peer(e):
        return lax.rem(mine + e, n_m)

    def p_peer(q):
        return lax.rem(lane + q, n_p)

    barrier = pltpu.get_barrier_semaphore()

    def greet(axis, peer):
        pl.semaphore_signal(barrier, inc=1, device_id={axis: peer}, device_id_type=MESH)

    loop(n_b - 1, lambda i: greet("bond", b_peer(i + 1)))
    loop(n_m - 1, lambda i: greet("mpo", m_peer(i + 1)))
    loop(n_p - 1, lambda i: greet("phys", p_peer(i + 1)))
    pl.semaphore_wait(barrier, n_b + n_m + n_p - 3)

    def remote(src, dst, send, recv, axis, peer):
        return pltpu.make_async_remote_copy(
            src_ref=src,
            dst_ref=dst,
            send_sem=send,
            recv_sem=recv,
            device_id={axis: peer},
            device_id_type=MESH,
        )

    def spot(owner, part):
        return pl.ds(owner * rcount + part * piece, piece)

    def small(e):
        peer = m_peer(e)
        pairs = [
            (ops_ref, ops_all.at[e]),
            (pat_ref, pat_all.at[e]),
            (lmask_ref, lmask_all.at[e]),
            (rmask_ref, rmask_all.at[e]),
            (left_ref.at[:, :, pl.ds(peer * rows, rows)], left_v.at[e]),
        ]
        return [
            remote(s, d, small_send.at[e - 1, i], small_recv.at[e - 1, i], "mpo", peer)
            for i, (s, d) in enumerate(pairs)
        ]

    own_piece = right_ref.at[:, pl.ds(lane * piece, piece)]

    def z_copy(d):
        return remote(
            own_piece,
            right_own.at[:, spot(here, lane)],
            z_send.at[d - 1],
            z_recv.at[d - 1],
            "bond",
            b_peer(d),
        )

    def x_copy(d, e):
        owner = b_from(d)
        src = own_piece if isinstance(d, int) and d == 0 else right_own.at[:, spot(owner, lane)]
        return remote(
            src,
            right_oth.at[e - 1, :, spot(owner, lane)],
            x_send.at[e - 1, d],
            x_recv.at[e - 1, d],
            "mpo",
            m_peer(e),
        )

    def cz_copy(d, q):
        place = right_own.at[:, spot(b_from(d), lane)]
        return remote(
            place, place, cz_send.at[q - 1, d - 1], cz_recv.at[q - 1, d - 1], "phys", p_peer(q)
        )

    def cx_copy(d, e, q):
        place = right_oth.at[e - 1, :, spot(b_from(d), lane)]
        return remote(
            place,
            place,
            cx_send.at[q - 1, e - 1, d],
            cx_recv.at[q - 1, e - 1, d],
            "phys",
            p_peer(q),
        )

    smalls = [c for e in range(1, n_m) for c in small(e)]
    for copy in smalls:
        copy.start()
    for e in range(1, n_m):
        x_copy(0, e).start()
    loop(n_b - 1, lambda i: z_copy(i + 1).start())

    for copy in own_copies:
        copy.wait()
    for copy in smalls:
        copy.wait()

    row_at = mine * rows + lax.broadcasted_iota(jnp.int32, (rows, width), 0)
    col_at = lax.broadcasted_iota(jnp.int32, (rows, width), 1)
    for a in range(lcount):
        size = lsize[here * lcount + a]
        keep = jnp.logical_and(row_at < size, col_at < size)
        for e in range(n_m):
            for k in range(terms):
                on = lmask_all[e, k, here * lcount + a].astype(jnp.float32)
                value = left_v[e, k, a].astype(jnp.float32) * on
                left_all[a, pl.ds((e * terms + k) * rows, rows)] = jnp.where(
                    keep, value, 0.0
                ).astype(jnp.bfloat16)
    for e in range(n_m):
        for k in range(terms):
            for s in range(states):
                for t in range(states):
                    coef[((e * terms + k) * states + s) * states + t] = ops_all[
                        e, k, s, t
                    ] * pat_all[e, k, s, t].astype(jnp.float32)

    base = (here * n_p + lane) * blocks

    def column_keep(b):
        lanes = lax.broadcasted_iota(jnp.int32, (1, width), 1)
        return (lanes < rsize[b]).astype(jnp.float32)

    def left_block(j):
        a = lax.rem(lsec[base + j], lcount)
        b = rsec[base + j]
        keep = column_keep(b).astype(jnp.bfloat16)
        state = jnp.concatenate([psi_v[j, s] * keep for s in range(states)], axis=1)
        for g in range(n_m):
            product = jnp.dot(
                left_all[a, pl.ds(g * terms * rows, terms * rows)],
                state,
                preferred_element_type=jnp.float32,
            )
            for k in range(terms):
                on = rmask_all[g, k, b].astype(jnp.float32)
                at = g * terms + k
                for s in range(states):
                    total = None
                    for t in range(states):
                        weight = coef[(at * states + s) * states + t] * on
                        term = (
                            product[k * rows : (k + 1) * rows, t * width : (t + 1) * width]
                            * weight
                        )
                        total = term if total is None else total + term
                    mix[j, pl.ds(s * rows, rows), pl.ds(at * width, width)] = total.astype(
                        jnp.bfloat16
                    )

    def forward(d):
        z_copy(d).wait_recv()
        for e in range(1, n_m):
            x_copy(d, e).start()
        for q in range(1, n_p):
            cz_copy(d, q).start()

    def forward_x(d):
        for e in range(1, n_m):
            x_copy(d, e).wait_recv()
            for q in range(1, n_p):
                cx_copy(d, e, q).start()

    def left_chunk(c):
        psi_copies[c].wait()
        lax.fori_loop(c * per, (c + 1) * per, lambda j, carry: (left_block(j), carry)[1], 0, unroll=2)

    for c in range(chunks):
        left_chunk(c)
        if n_b <= 8 and c < n_b - 1:
            forward(c + 1)
    if n_b <= 8:
        for d in range(chunks + 1, n_b):
            forward(d)
    else:
        lax.fori_loop(1, n_b, lambda d, carry: (forward(d), carry)[1], 0)

    forward_x(0)

    def own_ready(d):
        for q in range(1, n_p):
            cz_copy(d, q).wait()

    loop(n_b - 1, lambda i: own_ready(i + 1))

    def right_own_block(j, carry):
        b = rsec[base + j]
        weights = jnp.concatenate([right_own[k, b] for k in range(terms)], axis=0)
        acc[j] = jnp.dot(
            mix[j, :, pl.ds(0, terms * width)], weights, preferred_element_type=jnp.float32
        )
        return carry

    lax.fori_loop(0, blocks, right_own_block, 0, unroll=2)

    loop(n_b - 1, lambda i: forward_x(i + 1))

    def oth_ready(d):
        for e in range(1, n_m):
            for q in range(1, n_p):
                cx_copy(d, e, q).wait()

    loop(n_b, oth_ready)

    def out_copy(j):
        return pltpu.make_async_copy(out_v.at[j], out_ref.at[j], out_sem.at[j])

    def right_oth_block(j, carry):
        b = rsec[base + j]
        total = acc[j]
        for e in range(1, n_m):
            weights = jnp.concatenate([right_oth[e - 1, k, b] for k in range(terms)], axis=0)
            total = total + jnp.dot(
                mix[j, :, pl.ds(e * terms * width, terms * width)],
                weights,
                preferred_element_type=jnp.float32,
            )
        total = (total * column_keep(b)).astype(jnp.bfloat16)
        for s in range(states):
            out_v[j, s] = total[s * rows : (s + 1) * rows]
        out_copy(j).start()
        return carry

    lax.fori_loop(0, blocks, right_oth_block, 0, unroll=2)

    def sent(d):
        z_copy(d).wait_send()

    loop(n_b - 1, lambda i: sent(i + 1))

    def sent_x(d):
        for e in range(1, n_m):
            x_copy(d, e).wait_send()

    loop(n_b, sent_x)
    lax.fori_loop(0, blocks, lambda j, carry: (out_copy(j).wait(), carry)[1], 0)


def shards(
    psi,
    left_env,
    right_env,
    mpo_ops,
    mpo_pattern,
    left_mask,
    right_mask,
    left_sector,
    right_sector,
    left_size,
    right_size,
):
    blocks, states, width, _ = psi.shape
    terms, lcount = left_env.shape[:2]
    rcount = right_env.shape[1]
    n_b, n_m, n_p = (lax.axis_size(a) for a in ("bond", "mpo", "phys"))
    rows = width // n_m
    sectors = n_b * rcount
    lefts = left_size.shape[0]
    bf16, f32, i32 = jnp.bfloat16, jnp.float32, jnp.int32
    chunks = 4
    dma = pltpu.SemaphoreType.DMA
    anyspace = pl.BlockSpec(memory_space=pl.ANY)
    smem = pl.BlockSpec(memory_space=pltpu.SMEM)
    return pl.pallas_call(
        functools.partial(kernel, (n_b, n_m, n_p)),
        out_shape=jax.ShapeDtypeStruct((blocks, states, rows, width), bf16),
        in_specs=[anyspace] * 7 + [smem] * 4,
        out_specs=anyspace,
        scratch_shapes=[
            pltpu.VMEM((blocks, states, width, width), bf16),
            pltpu.VMEM((n_m, terms, lcount, rows, width), bf16),
            pltpu.VMEM((lcount, n_m * terms * rows, width), bf16),
            pltpu.VMEM((terms, sectors, width, width), bf16),
            pltpu.VMEM((n_m - 1, terms, sectors, width, width), bf16),
            pltpu.VMEM((blocks, states * rows, n_m * terms * width), bf16),
            pltpu.VMEM((blocks, states * rows, width), f32),
            pltpu.VMEM((blocks, states, rows, width), bf16),
            pltpu.SMEM((n_m, terms, states, states), f32),
            pltpu.SMEM((n_m, terms, states, states), i32),
            pltpu.SMEM((n_m, terms, lefts), i32),
            pltpu.SMEM((n_m, terms, sectors), i32),
            pltpu.SMEM((n_m * terms * states * states,), f32),
            dma((chunks,)),
            dma((blocks,)),
            dma((6,)),
            dma((n_m - 1, 5)),
            dma((n_m - 1, 5)),
            dma((n_b - 1,)),
            dma((n_b - 1,)),
            dma((n_m - 1, n_b)),
            dma((n_m - 1, n_b)),
            dma((n_p - 1, n_b - 1)),
            dma((n_p - 1, n_b - 1)),
            dma((n_p - 1, n_m - 1, n_b)),
            dma((n_p - 1, n_m - 1, n_b)),
        ],
        compiler_params=pltpu.CompilerParams(
            collective_id=0, has_side_effects=True, vmem_limit_bytes=56 * 1024 * 1024
        ),
    )(
        psi,
        left_env,
        right_env,
        mpo_ops,
        mpo_pattern,
        left_mask,
        right_mask,
        left_sector,
        right_sector,
        left_size,
        right_size,
    )


def solution(mesh):
    placed = (
        P(("groups", "bond", "phys"), None, None, None),
        P("mpo", ("groups", "bond"), None, None),
        P("mpo", ("groups", "bond"), None, None),
        P("mpo", None, None),
        P("mpo", None, None),
        P("mpo", "groups"),
        P("mpo", "groups"),
        P("groups"),
        P("groups"),
        P("groups"),
        P("groups"),
    )
    return jax.shard_map(
        shards,
        mesh=mesh,
        in_specs=placed,
        out_specs=P(("groups", "bond", "phys"), None, "mpo", None),
        check_vma=False,
    )
```

```python
import functools

import jax
import jax.numpy as jnp
from jax import lax
from jax.experimental import pallas as pl
from jax.experimental.pallas import tpu as pltpu
from jax.sharding import PartitionSpec as P

MESH = pl.DeviceIdType.MESH


def loop(count, body):
    if count <= 8:
        for index in range(count):
            body(index)
    else:
        lax.fori_loop(0, count, lambda i, c: (body(i), c)[1], 0)


def kernel(
    sizes,
    psi_ref,
    left_ref,
    right_ref,
    ops_ref,
    pat_ref,
    lmask_ref,
    rmask_ref,
    lsec_ref,
    rsec_ref,
    lsize_ref,
    rsize_ref,
    out_ref,
    psi_v,
    left_v,
    left_all,
    right_own,
    mix,
    acc,
    out_v,
    ops_all,
    pat_all,
    lmask_all,
    rmask_all,
    coef,
    lsec,
    rsec,
    lsize,
    rsize,
    psi_sem,
    out_sem,
    own_sem,
    small_send,
    small_recv,
    z_send,
    z_recv,
    x_send,
    x_recv,
    cz_send,
    cz_recv,
    cx_send,
    cx_recv,
    *right_oth,
):
    n_b, n_m, n_p = sizes
    blocks, states, width, _ = psi_ref.shape
    terms = left_ref.shape[0]
    lcount = left_ref.shape[1]
    rcount = right_ref.shape[1]
    rows = width // n_m
    piece = rcount // n_p
    here = lax.axis_index("bond")
    mine = lax.axis_index("mpo")
    lane = lax.axis_index("phys")
    chunks = psi_sem.shape[0]
    per = blocks // chunks

    psi_copies = [
        pltpu.make_async_copy(
            psi_ref.at[pl.ds(c * per, per)], psi_v.at[pl.ds(c * per, per)], psi_sem.at[c]
        )
        for c in range(chunks)
    ]
    own_copies = [
        pltpu.make_async_copy(
            left_ref.at[:, :, pl.ds(mine * rows, rows)], left_v.at[0], own_sem.at[0]
        ),
        pltpu.make_async_copy(
            right_ref, right_own.at[:, pl.ds(here * rcount, rcount)], own_sem.at[1]
        ),
        pltpu.make_async_copy(ops_ref, ops_all.at[0], own_sem.at[2]),
        pltpu.make_async_copy(pat_ref, pat_all.at[0], own_sem.at[3]),
        pltpu.make_async_copy(lmask_ref, lmask_all.at[0], own_sem.at[4]),
        pltpu.make_async_copy(rmask_ref, rmask_all.at[0], own_sem.at[5]),
        pltpu.make_async_copy(lsec_ref, lsec, own_sem.at[6]),
        pltpu.make_async_copy(rsec_ref, rsec, own_sem.at[7]),
        pltpu.make_async_copy(lsize_ref, lsize, own_sem.at[8]),
        pltpu.make_async_copy(rsize_ref, rsize, own_sem.at[9]),
    ]
    line = n_b == 4

    def b_peer(d):
        if line:
            return (here, here + 1 - 2 * lax.rem(here, 2), lax.rem(here + 2, 4), 3 - here)[d]
        return lax.rem(here + d, n_b)

    def b_from(d):
        if line:
            return b_peer(d)
        return lax.rem(here + n_b - d, n_b)

    def m_peer(e):
        return lax.rem(mine + e, n_m)

    def p_peer(q):
        return lax.rem(lane + q, n_p)

    barrier = pltpu.get_barrier_semaphore()

    def greet(axis, peer):
        pl.semaphore_signal(barrier, inc=1, device_id={axis: peer}, device_id_type=MESH)

    loop(n_b - 1, lambda i: greet("bond", b_peer(i + 1)))
    loop(n_m - 1, lambda i: greet("mpo", m_peer(i + 1)))
    loop(n_p - 1, lambda i: greet("phys", p_peer(i + 1)))
    for copy in own_copies + psi_copies:
        copy.start()
    pl.semaphore_wait(barrier, n_b + n_m + n_p - 3)

    def remote(src, dst, send, recv, axis, peer):
        return pltpu.make_async_remote_copy(
            src_ref=src,
            dst_ref=dst,
            send_sem=send,
            recv_sem=recv,
            device_id={axis: peer},
            device_id_type=MESH,
        )

    def spot(owner, part):
        return pl.ds(owner * rcount + part * piece, piece)

    def small(e):
        peer = m_peer(e)
        pairs = [
            (ops_ref, ops_all.at[e]),
            (pat_ref, pat_all.at[e]),
            (lmask_ref, lmask_all.at[e]),
            (rmask_ref, rmask_all.at[e]),
            (left_ref.at[:, :, pl.ds(peer * rows, rows)], left_v.at[e]),
        ]
        return [
            remote(s, d, small_send.at[e - 1, i], small_recv.at[e - 1, i], "mpo", peer)
            for i, (s, d) in enumerate(pairs)
        ]

    def own_piece(t):
        return right_ref.at[t, pl.ds(lane * piece, piece)]

    def z_copy(d, t):
        return remote(
            own_piece(t),
            right_own.at[t, spot(here, lane)],
            z_send.at[d - 1, t],
            z_recv.at[d - 1, t],
            "bond",
            b_peer(d),
        )

    def z_relay(t):
        place = right_own.at[t, spot(b_from(3), lane)]
        return remote(place, place, z_send.at[1, t], z_recv.at[1, t], "bond", b_peer(1))

    def x_copy(d, e, t):
        owner = b_from(d)
        own = isinstance(d, int) and d == 0
        src = own_piece(t) if own else right_own.at[t, spot(owner, lane)]
        return remote(
            src,
            right_oth[t].at[e - 1, spot(owner, lane)],
            x_send.at[e - 1, d, t],
            x_recv.at[e - 1, d, t],
            "mpo",
            m_peer(e),
        )

    def cz_copy(d, q, t):
        place = right_own.at[t, spot(b_from(d), lane)]
        return remote(
            place,
            place,
            cz_send.at[q - 1, d - 1, t],
            cz_recv.at[q - 1, d - 1, t],
            "phys",
            p_peer(q),
        )

    def cx_copy(d, e, q, t):
        place = right_oth[t].at[e - 1, spot(b_from(d), lane)]
        return remote(
            place,
            place,
            cx_send.at[q - 1, e - 1, d, t],
            cx_recv.at[q - 1, e - 1, d, t],
            "phys",
            p_peer(q),
        )

    smalls = [c for e in range(1, n_m) for c in small(e)]
    middle = jnp.logical_and(here > 0, here < n_b - 1)
    for copy in smalls:
        copy.start()
    for t in range(terms):
        for e in range(1, n_m):
            x_copy(0, e, t).start()
        if line:

            def send_middle(t=t):
                z_copy(3, t).start()
                z_copy(1, t).start()

            def send_end(t=t):
                for d in (1, 2, 3):
                    z_copy(d, t).start()

            pl.when(middle)(send_middle)
            pl.when(jnp.logical_not(middle))(send_end)
        else:
            loop(n_b - 1, lambda i, t=t: z_copy(i + 1, t).start())

    for copy in own_copies:
        copy.wait()
    for copy in smalls:
        copy.wait()

    row_at = mine * rows + lax.broadcasted_iota(jnp.int32, (rows, width), 0)
    col_at = lax.broadcasted_iota(jnp.int32, (rows, width), 1)
    for a in range(lcount):
        size = lsize[here * lcount + a]
        keep = jnp.logical_and(row_at < size, col_at < size)
        for e in range(n_m):
            for k in range(terms):
                on = lmask_all[e, k, here * lcount + a].astype(jnp.float32)
                value = left_v[e, k, a].astype(jnp.float32) * on
                left_all[a, pl.ds((e * terms + k) * rows, rows)] = jnp.where(
                    keep, value, 0.0
                ).astype(jnp.bfloat16)
    for e in range(n_m):
        for k in range(terms):
            for s in range(states):
                for t in range(states):
                    coef[((e * terms + k) * states + s) * states + t] = ops_all[
                        e, k, s, t
                    ] * pat_all[e, k, s, t].astype(jnp.float32)

    base = (here * n_p + lane) * blocks

    def column_keep(b):
        lanes = lax.broadcasted_iota(jnp.int32, (1, width), 1)
        return (lanes < rsize[b]).astype(jnp.float32)

    def left_block(j):
        a = lax.rem(lsec[base + j], lcount)
        b = rsec[base + j]
        keep = column_keep(b).astype(jnp.bfloat16)
        state = jnp.concatenate([psi_v[j, s] * keep for s in range(states)], axis=1)
        for g in range(n_m):
            product = jnp.dot(
                left_all[a, pl.ds(g * terms * rows, terms * rows)],
                state,
                preferred_element_type=jnp.float32,
            )
            for k in range(terms):
                on = rmask_all[g, k, b].astype(jnp.float32)
                at = g * terms + k
                for s in range(states):
                    total = None
                    for t in range(states):
                        weight = coef[(at * states + s) * states + t] * on
                        term = (
                            product[k * rows : (k + 1) * rows, t * width : (t + 1) * width]
                            * weight
                        )
                        total = term if total is None else total + term
                    mix[j, pl.ds(s * rows, rows), pl.ds(at * width, width)] = total.astype(
                        jnp.bfloat16
                    )

    def forward(d, t):
        z_copy(d, t).wait_recv()
        if line and d == 3:
            pl.when(middle)(lambda: z_relay(t).start())
        for e in range(1, n_m):
            x_copy(d, e, t).start()
        for q in range(1, n_p):
            cz_copy(d, q, t).start()

    def forward_x(d, t):
        for e in range(1, n_m):
            x_copy(d, e, t).wait_recv()
            for q in range(1, n_p):
                cx_copy(d, e, q, t).start()

    def left_chunk(c):
        psi_copies[c].wait()
        lax.fori_loop(c * per, (c + 1) * per, lambda j, carry: (left_block(j), carry)[1], 0, unroll=2)

    if line:
        steps = [lambda d=d, t=t: forward(d, t) for t in range(terms) for d in (1, 3, 2)]
    else:
        steps = [
            lambda t=t: loop(n_b - 1, lambda i: forward(i + 1, t)) for t in range(terms)
        ]
    for c in range(chunks):
        left_chunk(c)
        if steps:
            steps.pop(0)()
    for t in range(terms):
        forward_x(0, t)
    for step in steps:
        step()

    def own_ready(d):
        for q in range(1, n_p):
            for t in range(terms):
                cz_copy(d, q, t).wait()

    def oth_forward(t):
        if line:
            for d in (1, 3, 2):
                forward_x(d, t)
        else:
            loop(n_b - 1, lambda i: forward_x(i + 1, t))

    def oth_ready(t):
        def one(d):
            for e in range(1, n_m):
                for q in range(1, n_p):
                    cx_copy(d, e, q, t).wait()

        loop(n_b, one)

    loop(n_b - 1, lambda i: own_ready(i + 1))

    def right_own_block(j, carry):
        b = rsec[base + j]
        weights = jnp.concatenate([right_own[k, b] for k in range(terms)], axis=0)
        acc[j] = jnp.dot(
            mix[j, :, pl.ds(0, terms * width)], weights, preferred_element_type=jnp.float32
        )
        return carry

    lax.fori_loop(0, blocks, right_own_block, 0, unroll=2)

    def out_copy(j):
        return pltpu.make_async_copy(out_v.at[j], out_ref.at[j], out_sem.at[j])

    def oth_total(j, b, t):
        total = acc[j]
        for e in range(1, n_m):
            total = total + jnp.dot(
                mix[j, :, pl.ds((e * terms + t) * width, width)],
                right_oth[t][e - 1, b],
                preferred_element_type=jnp.float32,
            )
        return total

    def right_oth_block(t, j, carry):
        b = rsec[base + j]
        total = oth_total(j, b, t)
        if t < terms - 1:
            acc[j] = total
            return carry
        total = (total * column_keep(b)).astype(jnp.bfloat16)
        for s in range(states):
            out_v[j, s] = total[s * rows : (s + 1) * rows]
        out_copy(j).start()
        return carry

    for t in range(terms):
        oth_forward(t)
        oth_ready(t)
        lax.fori_loop(0, blocks, functools.partial(right_oth_block, t), 0, unroll=2)

    def sent(d):
        for t in range(terms):
            z_copy(d, t).wait_send()

    loop(n_b - 1, lambda i: sent(i + 1))

    def sent_x(d):
        for t in range(terms):
            for e in range(1, n_m):
                x_copy(d, e, t).wait_send()

    loop(n_b, sent_x)
    lax.fori_loop(0, blocks, lambda j, carry: (out_copy(j).wait(), carry)[1], 0)


def shards(
    psi,
    left_env,
    right_env,
    mpo_ops,
    mpo_pattern,
    left_mask,
    right_mask,
    left_sector,
    right_sector,
    left_size,
    right_size,
):
    blocks, states, width, _ = psi.shape
    terms, lcount = left_env.shape[:2]
    rcount = right_env.shape[1]
    n_b, n_m, n_p = (lax.axis_size(a) for a in ("bond", "mpo", "phys"))
    rows = width // n_m
    sectors = n_b * rcount
    lefts = left_size.shape[0]
    bf16, f32, i32 = jnp.bfloat16, jnp.float32, jnp.int32
    chunks = 4
    dma = pltpu.SemaphoreType.DMA
    anyspace = pl.BlockSpec(memory_space=pl.ANY)
    return pl.pallas_call(
        functools.partial(kernel, (n_b, n_m, n_p)),
        out_shape=jax.ShapeDtypeStruct((blocks, states, rows, width), bf16),
        in_specs=[anyspace] * 11,
        out_specs=anyspace,
        scratch_shapes=[
            pltpu.VMEM((blocks, states, width, width), bf16),
            pltpu.VMEM((n_m, terms, lcount, rows, width), bf16),
            pltpu.VMEM((lcount, n_m * terms * rows, width), bf16),
            pltpu.VMEM((terms, sectors, width, width), bf16),
            pltpu.VMEM((blocks, states * rows, n_m * terms * width), bf16),
            pltpu.VMEM((blocks, states * rows, width), f32),
            pltpu.VMEM((blocks, states, rows, width), bf16),
            pltpu.SMEM((n_m, terms, states, states), f32),
            pltpu.SMEM((n_m, terms, states, states), i32),
            pltpu.SMEM((n_m, terms, lefts), i32),
            pltpu.SMEM((n_m, terms, sectors), i32),
            pltpu.SMEM((n_m * terms * states * states,), f32),
            pltpu.SMEM(left_sector.shape, i32),
            pltpu.SMEM(right_sector.shape, i32),
            pltpu.SMEM(left_size.shape, i32),
            pltpu.SMEM(right_size.shape, i32),
            dma((chunks,)),
            dma((blocks,)),
            dma((10,)),
            dma((n_m - 1, 5)),
            dma((n_m - 1, 5)),
            dma((n_b - 1, terms)),
            dma((n_b - 1, terms)),
            dma((n_m - 1, n_b, terms)),
            dma((n_m - 1, n_b, terms)),
            dma((n_p - 1, n_b - 1, terms)),
            dma((n_p - 1, n_b - 1, terms)),
            dma((n_p - 1, n_m - 1, n_b, terms)),
            dma((n_p - 1, n_m - 1, n_b, terms)),
        ]
        + [pltpu.VMEM((n_m - 1, sectors, width, width), bf16) for _ in range(terms)],
        compiler_params=pltpu.CompilerParams(
            collective_id=0, has_side_effects=True, vmem_limit_bytes=56 * 1024 * 1024
        ),
    )(
        psi,
        left_env,
        right_env,
        mpo_ops,
        mpo_pattern,
        left_mask,
        right_mask,
        left_sector,
        right_sector,
        left_size,
        right_size,
    )


def solution(mesh):
    placed = (
        P(("groups", "bond", "phys"), None, None, None),
        P("mpo", ("groups", "bond"), None, None),
        P("mpo", ("groups", "bond"), None, None),
        P("mpo", None, None),
        P("mpo", None, None),
        P("mpo", "groups"),
        P("mpo", "groups"),
        P("groups"),
        P("groups"),
        P("groups"),
        P("groups"),
    )
    return jax.shard_map(
        shards,
        mesh=mesh,
        in_specs=placed,
        out_specs=P(("groups", "bond", "phys"), None, "mpo", None),
        check_vma=False,
    )
```

```python
import functools

import jax
import jax.numpy as jnp
from jax import lax
from jax.experimental import pallas as pl
from jax.experimental.pallas import tpu as pltpu
from jax.sharding import PartitionSpec as P

MESH = pl.DeviceIdType.MESH


def loop(count, body):
    if count <= 8:
        for index in range(count):
            body(index)
    else:
        lax.fori_loop(0, count, lambda i, c: (body(i), c)[1], 0)


def kernel(
    sizes,
    psi_ref,
    left_ref,
    right_ref,
    ops_ref,
    pat_ref,
    lmask_ref,
    rmask_ref,
    lsec_ref,
    rsec_ref,
    lsize_ref,
    rsize_ref,
    out_ref,
    psi_v,
    left_v,
    left_all,
    right_own,
    mix,
    acc,
    out_v,
    ops_all,
    pat_all,
    lmask_all,
    rmask_all,
    coef,
    lsec,
    rsec,
    lsize,
    rsize,
    psi_sem,
    out_sem,
    own_sem,
    small_send,
    small_recv,
    z_send,
    z_recv,
    x_send,
    x_recv,
    cz_send,
    cz_recv,
    cx_send,
    cx_recv,
    *right_oth,
):
    n_b, n_m, n_p = sizes
    blocks, states, width, _ = psi_ref.shape
    terms = left_ref.shape[0]
    lcount = left_ref.shape[1]
    rcount = right_ref.shape[1]
    rows = width // n_m
    piece = rcount // n_p
    here = lax.axis_index("bond")
    mine = lax.axis_index("mpo")
    lane = lax.axis_index("phys")
    chunks = psi_sem.shape[0]
    per = blocks // chunks

    psi_copies = [
        pltpu.make_async_copy(
            psi_ref.at[pl.ds(c * per, per)], psi_v.at[pl.ds(c * per, per)], psi_sem.at[c]
        )
        for c in range(chunks)
    ]
    own_copies = [
        pltpu.make_async_copy(
            left_ref.at[:, :, pl.ds(mine * rows, rows)], left_v.at[0], own_sem.at[0]
        ),
        pltpu.make_async_copy(
            right_ref, right_own.at[:, pl.ds(here * rcount, rcount)], own_sem.at[1]
        ),
        pltpu.make_async_copy(ops_ref, ops_all.at[0], own_sem.at[2]),
        pltpu.make_async_copy(pat_ref, pat_all.at[0], own_sem.at[3]),
        pltpu.make_async_copy(lmask_ref, lmask_all.at[0], own_sem.at[4]),
        pltpu.make_async_copy(rmask_ref, rmask_all.at[0], own_sem.at[5]),
        pltpu.make_async_copy(lsec_ref, lsec, own_sem.at[6]),
        pltpu.make_async_copy(rsec_ref, rsec, own_sem.at[7]),
        pltpu.make_async_copy(lsize_ref, lsize, own_sem.at[8]),
        pltpu.make_async_copy(rsize_ref, rsize, own_sem.at[9]),
    ]
    line = n_b == 4

    def b_peer(d):
        if line:
            return (here, here + 1 - 2 * lax.rem(here, 2), lax.rem(here + 2, 4), 3 - here)[d]
        return lax.rem(here + d, n_b)

    def b_from(d):
        if line:
            return b_peer(d)
        return lax.rem(here + n_b - d, n_b)

    def m_peer(e):
        return lax.rem(mine + e, n_m)

    def p_peer(q):
        return lax.rem(lane + q, n_p)

    barrier = pltpu.get_barrier_semaphore()

    def greet(axis, peer):
        pl.semaphore_signal(barrier, inc=1, device_id={axis: peer}, device_id_type=MESH)

    loop(n_b - 1, lambda i: greet("bond", b_peer(i + 1)))
    loop(n_m - 1, lambda i: greet("mpo", m_peer(i + 1)))
    loop(n_p - 1, lambda i: greet("phys", p_peer(i + 1)))
    for copy in own_copies + psi_copies:
        copy.start()
    pl.semaphore_wait(barrier, n_b + n_m + n_p - 3)

    def remote(src, dst, send, recv, axis, peer):
        return pltpu.make_async_remote_copy(
            src_ref=src,
            dst_ref=dst,
            send_sem=send,
            recv_sem=recv,
            device_id={axis: peer},
            device_id_type=MESH,
        )

    def spot(owner, part):
        return pl.ds(owner * rcount + part * piece, piece)

    def small(e):
        peer = m_peer(e)
        pairs = [
            (ops_ref, ops_all.at[e]),
            (pat_ref, pat_all.at[e]),
            (lmask_ref, lmask_all.at[e]),
            (rmask_ref, rmask_all.at[e]),
            (left_ref.at[:, :, pl.ds(peer * rows, rows)], left_v.at[e]),
        ]
        return [
            remote(s, d, small_send.at[e - 1, i], small_recv.at[e - 1, i], "mpo", peer)
            for i, (s, d) in enumerate(pairs)
        ]

    def own_piece(t):
        return right_ref.at[t, pl.ds(lane * piece, piece)]

    def z_copy(d, t):
        return remote(
            own_piece(t),
            right_own.at[t, spot(here, lane)],
            z_send.at[d - 1, t],
            z_recv.at[d - 1, t],
            "bond",
            b_peer(d),
        )

    def z_relay(t):
        place = right_own.at[t, spot(b_from(3), lane)]
        return remote(place, place, z_send.at[1, t], z_recv.at[1, t], "bond", b_peer(1))

    def x_copy(d, e, t):
        owner = b_from(d)
        own = isinstance(d, int) and d == 0
        src = own_piece(t) if own else right_own.at[t, spot(owner, lane)]
        return remote(
            src,
            right_oth[t].at[e - 1, spot(owner, lane)],
            x_send.at[e - 1, d, t],
            x_recv.at[e - 1, d, t],
            "mpo",
            m_peer(e),
        )

    def cz_copy(d, q, t):
        place = right_own.at[t, spot(b_from(d), lane)]
        return remote(
            place,
            place,
            cz_send.at[q - 1, d - 1, t],
            cz_recv.at[q - 1, d - 1, t],
            "phys",
            p_peer(q),
        )

    def cx_copy(d, e, q, t):
        place = right_oth[t].at[e - 1, spot(b_from(d), lane)]
        return remote(
            place,
            place,
            cx_send.at[q - 1, e - 1, d, t],
            cx_recv.at[q - 1, e - 1, d, t],
            "phys",
            p_peer(q),
        )

    smalls = [c for e in range(1, n_m) for c in small(e)]
    middle = jnp.logical_and(here > 0, here < n_b - 1)
    for copy in smalls:
        copy.start()
    for t in range(terms):
        for e in range(1, n_m):
            x_copy(0, e, t).start()
        if line:

            def send_middle(t=t):
                z_copy(3, t).start()
                z_copy(1, t).start()

            def send_end(t=t):
                for d in (1, 2, 3):
                    z_copy(d, t).start()

            pl.when(middle)(send_middle)
            pl.when(jnp.logical_not(middle))(send_end)
        else:
            loop(n_b - 1, lambda i, t=t: z_copy(i + 1, t).start())

    for copy in own_copies:
        copy.wait()
    for copy in smalls:
        copy.wait()

    row_at = mine * rows + lax.broadcasted_iota(jnp.int32, (rows, width), 0)
    col_at = lax.broadcasted_iota(jnp.int32, (rows, width), 1)
    for a in range(lcount):
        size = lsize[here * lcount + a]
        keep = jnp.logical_and(row_at < size, col_at < size)
        for e in range(n_m):
            for k in range(terms):
                on = lmask_all[e, k, here * lcount + a].astype(jnp.float32)
                value = left_v[e, k, a].astype(jnp.float32) * on
                left_all[a, pl.ds((e * terms + k) * rows, rows)] = jnp.where(
                    keep, value, 0.0
                ).astype(jnp.bfloat16)
    for e in range(n_m):
        for k in range(terms):
            for s in range(states):
                for t in range(states):
                    coef[((e * terms + k) * states + s) * states + t] = ops_all[
                        e, k, s, t
                    ] * pat_all[e, k, s, t].astype(jnp.float32)

    base = (here * n_p + lane) * blocks

    def column_keep(b):
        lanes = lax.broadcasted_iota(jnp.int32, (1, width), 1)
        return (lanes < rsize[b]).astype(jnp.float32)

    def left_block(j):
        a = lax.rem(lsec[base + j], lcount)
        b = rsec[base + j]
        keep = column_keep(b).astype(jnp.bfloat16)
        state = jnp.concatenate([psi_v[j, s] * keep for s in range(states)], axis=1)
        for g in range(n_m):
            product = jnp.dot(
                left_all[a, pl.ds(g * terms * rows, terms * rows)],
                state,
                preferred_element_type=jnp.float32,
            )
            for k in range(terms):
                on = rmask_all[g, k, b].astype(jnp.float32)
                at = g * terms + k
                for s in range(states):
                    total = None
                    for t in range(states):
                        weight = coef[(at * states + s) * states + t] * on
                        term = (
                            product[k * rows : (k + 1) * rows, t * width : (t + 1) * width]
                            * weight
                        )
                        total = term if total is None else total + term
                    mix[j, pl.ds(s * rows, rows), pl.ds(at * width, width)] = total.astype(
                        jnp.bfloat16
                    )

    def forward(d, t):
        z_copy(d, t).wait_recv()
        if line and d == 3:
            pl.when(middle)(lambda: z_relay(t).start())
        for e in range(1, n_m):
            x_copy(d, e, t).start()
        for q in range(1, n_p):
            cz_copy(d, q, t).start()

    def forward_x(d, t):
        for e in range(1, n_m):
            x_copy(d, e, t).wait_recv()
            for q in range(1, n_p):
                cx_copy(d, e, q, t).start()

    def left_chunk(c):
        psi_copies[c].wait()
        lax.fori_loop(c * per, (c + 1) * per, lambda j, carry: (left_block(j), carry)[1], 0, unroll=2)

    if line:
        steps = [lambda d=d, t=t: forward(d, t) for t in range(terms) for d in (1, 3, 2)]
    else:
        steps = [
            lambda t=t: loop(n_b - 1, lambda i: forward(i + 1, t)) for t in range(terms)
        ]
    for c in range(chunks):
        left_chunk(c)
        if steps:
            steps.pop(0)()
    for t in range(terms):
        forward_x(0, t)
    for step in steps:
        step()

    def own_ready(d):
        for q in range(1, n_p):
            for t in range(terms):
                cz_copy(d, q, t).wait()

    def oth_forward(t):
        if line:
            for d in (1, 3, 2):
                forward_x(d, t)
        else:
            loop(n_b - 1, lambda i: forward_x(i + 1, t))

    def oth_ready(t):
        def one(d):
            for e in range(1, n_m):
                for q in range(1, n_p):
                    cx_copy(d, e, q, t).wait()

        loop(n_b, one)

    oth_forward(0)
    loop(n_b - 1, lambda i: own_ready(i + 1))

    def right_own_block(j, carry):
        b = rsec[base + j]
        weights = jnp.concatenate([right_own[k, b] for k in range(terms)], axis=0)
        acc[j] = jnp.dot(
            mix[j, :, pl.ds(0, terms * width)], weights, preferred_element_type=jnp.float32
        )
        return carry

    lax.fori_loop(0, blocks, right_own_block, 0, unroll=4)

    def out_copy(j):
        return pltpu.make_async_copy(out_v.at[j], out_ref.at[j], out_sem.at[j])

    def oth_total(j, b, t):
        total = acc[j]
        for e in range(1, n_m):
            total = total + jnp.dot(
                mix[j, :, pl.ds((e * terms + t) * width, width)],
                right_oth[t][e - 1, b],
                preferred_element_type=jnp.float32,
            )
        return total

    def right_oth_block(t, j, carry):
        b = rsec[base + j]
        total = oth_total(j, b, t)
        if t < terms - 1:
            acc[j] = total
            return carry
        total = (total * column_keep(b)).astype(jnp.bfloat16)
        for s in range(states):
            out_v[j, s] = total[s * rows : (s + 1) * rows]
        out_copy(j).start()
        return carry

    for t in range(terms):
        if t > 0:
            oth_forward(t)
        oth_ready(t)
        lax.fori_loop(0, blocks, functools.partial(right_oth_block, t), 0, unroll=4)

    def sent(d):
        for t in range(terms):
            z_copy(d, t).wait_send()

    loop(n_b - 1, lambda i: sent(i + 1))

    def sent_x(d):
        for t in range(terms):
            for e in range(1, n_m):
                x_copy(d, e, t).wait_send()

    loop(n_b, sent_x)
    lax.fori_loop(0, blocks, lambda j, carry: (out_copy(j).wait(), carry)[1], 0)


def place(parts, src, dst, buf, sem, sem2):
    step = src.shape[0] // parts
    ins = [
        pltpu.make_async_copy(
            src.at[pl.ds(c * step, step)], buf.at[pl.ds(c * step, step)], sem.at[c]
        )
        for c in range(parts)
    ]
    outs = [
        pltpu.make_async_copy(
            buf.at[pl.ds(c * step, step)], dst.at[pl.ds(c * step, step)], sem2.at[c]
        )
        for c in range(parts)
    ]
    for copy in ins:
        copy.start()
    for a, b in zip(ins, outs):
        a.wait()
        b.start()
    for copy in outs:
        copy.wait()


def shards(
    psi,
    left_env,
    right_env,
    mpo_ops,
    mpo_pattern,
    left_mask,
    right_mask,
    left_sector,
    right_sector,
    left_size,
    right_size,
):
    blocks, states, width, _ = psi.shape
    terms, lcount = left_env.shape[:2]
    rcount = right_env.shape[1]
    n_b, n_m, n_p = (lax.axis_size(a) for a in ("bond", "mpo", "phys"))
    rows = width // n_m
    sectors = n_b * rcount
    lefts = left_size.shape[0]
    bf16, f32, i32 = jnp.bfloat16, jnp.float32, jnp.int32
    chunks = 4
    dma = pltpu.SemaphoreType.DMA
    anyspace = pl.BlockSpec(memory_space=pl.ANY)
    h = pl.pallas_call(
        functools.partial(kernel, (n_b, n_m, n_p)),
        out_shape=jax.ShapeDtypeStruct((blocks, states, rows, width), bf16),
        in_specs=[anyspace] * 11,
        out_specs=anyspace,
        scratch_shapes=[
            pltpu.VMEM((blocks, states, width, width), bf16),
            pltpu.VMEM((n_m, terms, lcount, rows, width), bf16),
            pltpu.VMEM((lcount, n_m * terms * rows, width), bf16),
            pltpu.VMEM((terms, sectors, width, width), bf16),
            pltpu.VMEM((blocks, states * rows, n_m * terms * width), bf16),
            pltpu.VMEM((blocks, states * rows, width), f32),
            pltpu.VMEM((blocks, states, rows, width), bf16),
            pltpu.SMEM((n_m, terms, states, states), f32),
            pltpu.SMEM((n_m, terms, states, states), i32),
            pltpu.SMEM((n_m, terms, lefts), i32),
            pltpu.SMEM((n_m, terms, sectors), i32),
            pltpu.SMEM((n_m * terms * states * states,), f32),
            pltpu.SMEM(left_sector.shape, i32),
            pltpu.SMEM(right_sector.shape, i32),
            pltpu.SMEM(left_size.shape, i32),
            pltpu.SMEM(right_size.shape, i32),
            dma((chunks,)),
            dma((blocks,)),
            dma((10,)),
            dma((n_m - 1, 5)),
            dma((n_m - 1, 5)),
            dma((n_b - 1, terms)),
            dma((n_b - 1, terms)),
            dma((n_m - 1, n_b, terms)),
            dma((n_m - 1, n_b, terms)),
            dma((n_p - 1, n_b - 1, terms)),
            dma((n_p - 1, n_b - 1, terms)),
            dma((n_p - 1, n_m - 1, n_b, terms)),
            dma((n_p - 1, n_m - 1, n_b, terms)),
        ]
        + [pltpu.VMEM((n_m - 1, sectors, width, width), bf16) for _ in range(terms)],
        compiler_params=pltpu.CompilerParams(
            collective_id=0, has_side_effects=True, vmem_limit_bytes=56 * 1024 * 1024
        ),
    )(
        psi,
        left_env,
        right_env,
        mpo_ops,
        mpo_pattern,
        left_mask,
        right_mask,
        left_sector,
        right_sector,
        left_size,
        right_size,
    )
    return pl.pallas_call(
        functools.partial(place, 8),
        out_shape=jax.ShapeDtypeStruct(h.shape, h.dtype),
        in_specs=[anyspace],
        out_specs=anyspace,
        scratch_shapes=[pltpu.VMEM(h.shape, h.dtype), dma((8,)), dma((8,))],
    )(h)


def solution(mesh):
    placed = (
        P(("groups", "bond", "phys"), None, None, None),
        P("mpo", ("groups", "bond"), None, None),
        P("mpo", ("groups", "bond"), None, None),
        P("mpo", None, None),
        P("mpo", None, None),
        P("mpo", "groups"),
        P("mpo", "groups"),
        P("groups"),
        P("groups"),
        P("groups"),
        P("groups"),
    )
    return jax.shard_map(
        shards,
        mesh=mesh,
        in_specs=placed,
        out_specs=P(("groups", "bond", "phys"), None, "mpo", None),
        check_vma=False,
    )
```
